256 devices in a mesh: section: 4 (over y), expert: 64 (over x, z, core).
Axes of the slice: x: 4, y: 4, z: 8, core: 2. Of those that a mesh axis runs over, the one named last changes fastest.
Arguments:
- tokens_in: bfloat16 [4, 2048, 3584], P('section', 'expert'), may hold values from -6 to 6
- cotangent: bfloat16 [4, 2048, 3584], P('section', 'expert'), may hold values from -6 to 6
- norm_gain: float32 [4, 3584], P('section'), may hold values from 0.1 to 1.9
- w_gate: bfloat16 [4, 64, 3584, 512], P('section', 'expert'), may hold values from -0.09375 to 0.09375
- w_up: bfloat16 [4, 64, 3584, 512], P('section', 'expert'), may hold values from -0.09375 to 0.09375
- w_down: bfloat16 [4, 64, 512, 3584], P('section', 'expert'), may hold values from -0.1875 to 0.1875
- expert_ids: int32 [4, 4, 2048, 1], P('section', None, 'expert'), may hold values from 0 to 31; in each aligned block of 32 rows (0 to 31, 32 to 63, ..., all dimensions but the last counted through in order) at most 2 rows name the same one
- gate_weights: float32 [4, 4, 2048, 1], P('section', None, 'expert'), may hold values from 0.2 to 1
Outputs:
- grad_inputs: bfloat16 [4, 4, 2048, 3584], P('section', None, 'expert')
- grad_gates: float32 [4, 4, 2048, 1], P('section', None, 'expert')
The draws below stay inside these ranges and needn't reach their ends.
Inputs may be any that keep to these rules, and one draw needn't show every extreme that they name: `expert_ids`: within each aligned block of 32 tokens of one layer and micro-batch no expert is named more than 2 times, a bound that some block reaches; each token names one expert.
All inputs are finite; a program needn't handle non-finite values.
Results may differ from the reference program's by a relative error of at most 0.025.
Values may be sent and summed in bfloat16 or wider, within the bound.
A program may use at most 192 MiB of HBM per device.

```python
import math
import jax
import jax.numpy as jnp
import numpy as np
from jax import lax

D = 3584
FF = 1024
TOP = 1
TOK_DEV = 32
EXPERTS = 32
FF_DEV = 512
CAP = 2
MICRO = 4
TOKENS = 2048
N_SECTION = 4
N_EXPERT = 64


def block_levels(stream_key, dims, cuts, smallest, largest):
    def one(dim, parts):
        heights = jax.random.uniform(jax.random.fold_in(jax.random.fold_in(stream_key, 6), dim), (parts,), jnp.float32, smallest / len(cuts), largest / len(cuts))
        return jnp.repeat(jnp.exp(heights), dims[dim] // parts).reshape((-1,) + (1,) * (len(dims) - dim - 1))

    loudness = one(*cuts[0])
    for cut in cuts[1:]:
        loudness = loudness * one(*cut)
    return loudness


def routed_block(key, own, number, rows, amount, top, bound, slope):
    ranking = jax.random.permutation(key, amount)
    crowded, common = load_shares(amount, rows * top, bound, slope, True), load_shares(amount, rows * top, bound, slope, False)
    places = jnp.arange(amount)

    def named(sizes, rotation):
        used = int((sizes > 0).sum())
        fixed = max(1, used // 4)
        passed = fixed + (places - fixed + rotation * (used - fixed)) % max(1, amount - fixed)
        return jnp.zeros((amount,), jnp.int32).at[ranking[jnp.where(places < fixed, places, passed)]].set(jnp.asarray(sizes, jnp.int32))

    sizes = jnp.where(number % 4 == 0, named(crowded, number // 4), named(common, number - number // 4 - 1))
    mixed = jax.random.permutation(jax.random.fold_in(own, 3), amount)
    giver, taker = mixed[0:amount // 2 * 2:2], mixed[1:amount // 2 * 2:2]
    slack = jnp.minimum(sizes[giver] - 1, bound - sizes[taker]) // 2
    slack = jnp.where((giver == ranking[0]) | (taker == ranking[0]) | (sizes[taker] == 0), 0, jnp.maximum(slack, 0))
    passed = jax.random.randint(jax.random.fold_in(own, 4), (amount // 2,), 0, 1 << 20) % (slack + 1)
    sizes = sizes.at[giver].add(-passed).at[taker].add(passed)
    items = jnp.searchsorted(jnp.cumsum(sizes), jnp.arange(rows * top), side="right").astype(jnp.int32)
    listing = items.reshape(top, rows).T
    listing = listing[jax.random.permutation(jax.random.fold_in(own, 1), rows)]
    rotation = jax.random.randint(jax.random.fold_in(own, 2), (rows, 1), 0, top)
    return jnp.take_along_axis(listing, (jnp.arange(top)[None, :] + rotation) % top, axis=1)


def load_shares(count, total, most, slope, full):
    weights = [(1 << 20) // math.isqrt(standing ** slope) + 1 for standing in range(1, count + 1)]
    largest = most if full else min(most, max(-(-total // count), total * weights[0] // sum(weights)))
    least = 1 if total - largest >= count - 1 else 0
    given, rest = [largest] + [least] * (count - 1), total - largest - least * (count - 1)
    while rest > 0:
        candidates = [i for i in range(1, count) if given[i] < largest] or [i for i in range(1, count) if given[i] < most]
        pool, remaining = sum([weights[i] for i in candidates]), rest
        for i in candidates:
            more = min(most - given[i], max(1, remaining * weights[i] // pool), rest)
            given[i] = given[i] + more
            rest = rest - more
    return np.array(given)


def normal_values(key, shape, width, most, pieces=(), kind=jnp.bfloat16):
    factor_of = block_levels(key, shape, pieces, -0.22, 0.18) if pieces else 1.0
    entries = jax.random.normal(key, shape, jnp.float32) * width * factor_of
    return jnp.minimum(jnp.maximum(entries, -most), most).astype(kind)


def setup_inputs(seed: int = 0) -> dict:
    key_list = jax.random.split(jax.random.key(seed), 9)
    tokens_in = normal_values(key_list[0], (MICRO, TOKENS, D), 1.0, 6.0, ((0, 4), (1, 64)))
    cotangent = normal_values(key_list[1], (MICRO, TOKENS, D), 1.0, 6.0, ((0, 4), (1, 64)))
    norm_gain = jnp.clip(1.0 + 0.18 * jax.random.normal(key_list[2], (N_SECTION, D), jnp.float32), 0.1, 1.9)
    w_gate = normal_values(key_list[3], (N_SECTION, N_EXPERT, D, FF_DEV), D ** -0.5, 0.09375, ((0, 4), (1, 64)))
    w_up = normal_values(key_list[4], (N_SECTION, N_EXPERT, D, FF_DEV), D ** -0.5, 0.09375, ((0, 4), (1, 64)))
    w_down = normal_values(key_list[5], (N_SECTION, N_EXPERT, FF_DEV, D), FF ** -0.5, 0.1875, ((0, 4), (1, 64)))
    expert_ids_keys = jax.random.split(jax.random.fold_in(key_list[6], 1), N_SECTION * MICRO * TOKENS // TOK_DEV)
    expert_ids_turns = jax.random.permutation(jax.random.fold_in(key_list[6], 3), N_SECTION * MICRO * TOKENS // TOK_DEV)
    expert_ids = jax.vmap(lambda own, number: routed_block(jax.random.fold_in(key_list[6], 2), own, number, TOK_DEV, EXPERTS, TOP, CAP, 1))(expert_ids_keys, expert_ids_turns).reshape((N_SECTION, MICRO, TOKENS, TOP))
    gate_weights = jnp.clip(0.2 + 0.8 * jax.random.uniform(key_list[7], (N_SECTION, MICRO, TOKENS, TOP), jnp.float32) ** block_levels(key_list[7], (N_SECTION, MICRO, TOKENS, TOP), ((0, 4), (2, 64)), -0.2, 0.2), 0.2, 1.0)
    return dict(tokens_in=tokens_in, cotangent=cotangent, norm_gain=norm_gain, w_gate=w_gate, w_up=w_up, w_down=w_down, expert_ids=expert_ids, gate_weights=gate_weights)


epsilon = 1e-06

def norm_rows(layer_in, gain_row):
    values = layer_in.astype(jnp.float32)
    inv_rms = lax.rsqrt(lax.optimization_barrier(jnp.mean(values * values, axis=-1, keepdims=True)) + epsilon)
    normed = (values * inv_rms * gain_row).astype(jnp.bfloat16)
    return (values, inv_rms, normed)

def slot_tables(route_ids):
    flat_ids = route_ids.reshape(N_EXPERT, TOK_DEV * TOP).astype(jnp.int32)
    one_hot = (flat_ids[:, :, None] == jnp.arange(EXPERTS, dtype=jnp.int32)[None, None, :]).astype(jnp.int32)
    position = lax.optimization_barrier(jnp.sum((jnp.cumsum(one_hot, axis=1, dtype=jnp.int32) - 1) * one_hot, axis=-1, dtype=jnp.int32))
    source = jnp.broadcast_to(jnp.arange(N_EXPERT, dtype=jnp.int32)[:, None], flat_ids.shape)
    return (flat_ids.reshape(-1), source.reshape(-1), position.reshape(-1))

def scatter_rows(row_block, expert_of, source, position):
    buffer = jnp.zeros((EXPERTS, N_EXPERT, CAP, D), row_block.dtype)
    buffer = buffer.at[expert_of, source, position].set(row_block)
    return buffer.reshape(EXPERTS, N_EXPERT * CAP, D)

def expert_forward(operands):
    row_block, gate_pair, up_pair, down_pair = operands
    total = jnp.zeros((row_block.shape[0], D), jnp.float32)
    for half_index in range(2):
        gate_pre = jnp.dot(row_block, gate_pair[half_index], preferred_element_type=jnp.float32)
        up_pre = jnp.dot(row_block, up_pair[half_index], preferred_element_type=jnp.float32)
        hidden = (jax.nn.silu(gate_pre) * up_pre).astype(jnp.bfloat16)
        half_out = jnp.dot(hidden, down_pair[half_index], preferred_element_type=jnp.float32).astype(jnp.bfloat16)
        total = total + lax.optimization_barrier(half_out).astype(jnp.float32)
    return total

def expert_backward(operands):
    row_block, grad_block, gate_pair, up_pair, down_pair = operands
    total = jnp.zeros((row_block.shape[0], D), jnp.float32)
    for half_index in range(2):
        gate_pre = jnp.dot(row_block, gate_pair[half_index], preferred_element_type=jnp.float32)
        up_pre = jnp.dot(row_block, up_pair[half_index], preferred_element_type=jnp.float32)
        sigma = jax.nn.sigmoid(gate_pre)
        grad_hidden = jnp.dot(grad_block, down_pair[half_index].T, preferred_element_type=jnp.float32)
        grad_gate = (grad_hidden * up_pre * sigma * (1.0 + gate_pre * (1.0 - sigma))).astype(jnp.bfloat16)
        grad_up = (grad_hidden * gate_pre * sigma).astype(jnp.bfloat16)
        half_grad = jnp.dot(grad_gate, gate_pair[half_index].T, preferred_element_type=jnp.float32)
        half_grad = half_grad + jnp.dot(grad_up, up_pair[half_index].T, preferred_element_type=jnp.float32)
        total = total + lax.optimization_barrier(half_grad.astype(jnp.bfloat16)).astype(jnp.float32)
    return total

def reference(tokens_in, cotangent, norm_gain, w_gate, w_up, w_down, expert_ids, gate_weights):
    gate_sets = [w_gate[layer].reshape(EXPERTS, 2, D, FF_DEV) for layer in range(N_SECTION)]
    up_sets = [w_up[layer].reshape(EXPERTS, 2, D, FF_DEV) for layer in range(N_SECTION)]
    down_sets = [w_down[layer].reshape(EXPERTS, 2, FF_DEV, D) for layer in range(N_SECTION)]
    grad_table = [[None] * MICRO for layer in range(N_SECTION)]
    gate_table = [[None] * MICRO for layer in range(N_SECTION)]
    for micro_index in range(MICRO):
        layer_in = tokens_in[micro_index]
        saved = []
        for layer in range(N_SECTION):
            values, inv_rms, normed = norm_rows(layer_in, norm_gain[layer])
            expert_of, source, position = slot_tables(expert_ids[layer, micro_index])
            dispatched = scatter_rows(jnp.repeat(normed, TOP, axis=0), expert_of, source, position)
            combined = lax.map(expert_forward, (dispatched, gate_sets[layer], up_sets[layer], down_sets[layer]))
            combined = combined.reshape(EXPERTS, N_EXPERT, CAP, D)
            expert_rows = combined[expert_of, source, position].reshape(TOKENS, TOP, D)
            mixed = lax.optimization_barrier(jnp.sum(gate_weights[layer, micro_index][:, :, None] * expert_rows, axis=1))
            saved.append((values, inv_rms, dispatched, expert_rows, expert_of, source, position))
            layer_in = (values + mixed).astype(jnp.bfloat16)
        grad_next = cotangent[micro_index]
        for layer in range(N_SECTION - 1, -1, -1):
            values, inv_rms, dispatched, expert_rows, expert_of, source, position = saved[layer]
            grad_f = grad_next.astype(jnp.float32)
            gate_table[layer][micro_index] = lax.optimization_barrier(jnp.sum(grad_f[:, None, :] * expert_rows, axis=-1))
            grad_rows = (gate_weights[layer, micro_index][:, :, None] * grad_f[:, None, :]).astype(jnp.bfloat16)
            grad_disp = scatter_rows(grad_rows.reshape(TOKENS * TOP, D), expert_of, source, position)
            returned = lax.map(expert_backward, (dispatched, grad_disp, gate_sets[layer], up_sets[layer], down_sets[layer]))
            returned = returned.reshape(EXPERTS, N_EXPERT, CAP, D)
            grad_norm = lax.optimization_barrier(jnp.sum(returned[expert_of, source, position].reshape(TOKENS, TOP, D), axis=1))
            scaled = grad_norm * norm_gain[layer]
            grad_in = grad_f + inv_rms * scaled - values * (inv_rms * inv_rms * inv_rms) * lax.optimization_barrier(jnp.mean(values * scaled, axis=-1, keepdims=True))
            grad_next = grad_in.astype(jnp.bfloat16)
            grad_table[layer][micro_index] = grad_next
    grad_inputs = jnp.stack([jnp.stack(grad_table[layer]) for layer in range(N_SECTION)])
    grad_gates = jnp.stack([jnp.stack(gate_table[layer]) for layer in range(N_SECTION)])
    return (grad_inputs, grad_gates)
```

```python
import functools

import jax
import jax.numpy as jnp
from jax import lax
from jax.experimental import pallas as pl
from jax.experimental.pallas import tpu as pltpu
from jax.sharding import PartitionSpec as P

MESH = pl.DeviceIdType.MESH
EPS = 1e-06
MICRO = 4
TOK = 32
CHIPS = 32
WIDTH = 3584
HALF = 512
ROWS = 2 * CHIPS
LANES = (512, 384)
STARTS = (0, 2048)
PARTS = len(LANES)
F32 = jnp.float32
BF16 = jnp.bfloat16
NT = (((1,), (1,)), ((), ()))
TILE = 256


def iota(shape, dim):
    return lax.broadcasted_iota(jnp.int32, shape, dim)


def kernel(
    tok_ref, cot_ref, gain_ref, wg_ref, wu_ref, wd_ref, idrow_ref, idcol_ref, gate_ref,
    gin_ref, ggate_ref,
    wg, wu, wd, place, pick, back,
    hbuf, gbuf, disp_f, disp_b, coll_f, coll_b, send_df, send_db, send_cf, send_cb,
    hsend, gsend, erows, hrows, gate_pre, up_pre, rms_all, acc_a, acc_b, act,
    w_send, w_recv, w_local, h_recv, g_recv, h_ssem, g_ssem,
    df_r, db_r, cf_r, cb_r, df_s, db_s, cf_s, cb_s,
):
    s, me = lax.axis_index("section"), lax.axis_index("expert")
    chip, core = me // 2, me % 2
    cx, cz = chip // 8, chip % 8
    sibling = me + 1 - 2 * core

    def peer(i):
        return (((cx + i // 8) % 4) * 8 + (cz + i % 8) % 8) * 2 + core

    local = []
    for n, (src, dst) in enumerate(((wg_ref, wg), (wu_ref, wu), (wd_ref, wd))):
        local.append(pltpu.make_async_copy(src.at[0, 0], dst.at[core], w_local.at[n]))
        local[-1].start()

    barrier = pltpu.get_barrier_semaphore()

    def greet(i, carry):
        pl.semaphore_signal(barrier, inc=1, device_id=(s, peer(i)), device_id_type=MESH)
        return carry

    lax.fori_loop(1, CHIPS, greet, 0)
    pl.semaphore_signal(barrier, inc=1, device_id=(s, sibling), device_id_type=MESH)
    for i in range(1, 4):
        pl.semaphore_signal(barrier, inc=1, device_id=((s + i) % 4, me), device_id_type=MESH)
    pl.semaphore_wait(barrier, CHIPS + 3)

    shared = []
    for n, (src, dst) in enumerate(((wg_ref, wg), (wu_ref, wu), (wd_ref, wd))):
        shared.append(
            pltpu.make_async_remote_copy(
                src.at[0, 0], dst.at[core], w_send.at[n], w_recv.at[n],
                device_id=(s, sibling), device_id_type=MESH,
            )
        )
        shared[-1].start()

    def stack(src, dst, p):
        w = LANES[p]
        for q in range(4):
            cols = slice(STARTS[p] + q * w, STARTS[p] + (q + 1) * w)
            dst[q * TOK : (q + 1) * TOK, :] = src[0, :, cols]

    def bring(src, stage, held, ssem, recv, p, owner):
        @pl.when(s == owner)
        def _():
            stack(src, held[p].at[owner], p)

        @pl.when(s != owner)
        def _():
            stack(src, stage[p], p)
            pltpu.make_async_remote_copy(
                stage[p], held[p].at[s], ssem.at[p], recv[p].at[s],
                device_id=(owner, me), device_id_type=MESH,
            ).start()

    for p in range(PARTS):
        bring(tok_ref, hsend, hbuf, h_ssem, h_recv, p, 0)
        bring(cot_ref, gsend, gbuf, g_ssem, g_recv, p, 3)

    def tables(m, carry):
        idrow, idcol = idrow_ref[m], idcol_ref[m]
        same = idcol == idrow
        ti, tj = iota((128, 128), 0), iota((128, 128), 1)
        before_row = same & (ti < TOK) & (ti < tj % TOK)
        before_col = same & (tj < TOK) & (tj < ti % TOK)
        slot_row = 2 * idrow + jnp.sum(before_row.astype(jnp.int32), axis=0, keepdims=True)
        slot_col = 2 * idcol + jnp.sum(before_col.astype(jnp.int32), axis=1, keepdims=True)
        r, c = iota((256, 128), 0), iota((256, 128), 1)
        hit = ((r // 8) * 2 + r % 2 == slot_row) & ((r // 2) % 4 == c // TOK)
        place[m] = hit.astype(F32).astype(BF16)
        r, c = iota((128, 256), 1), iota((128, 256), 0)
        hit = ((r // 8) * 2 + r % 2 == slot_col) & ((r // 2) % 4 == c // TOK)
        pick[m] = hit.astype(F32).astype(BF16)
        return carry

    lax.fori_loop(0, MICRO, tables, 0)
    r, c = iota((256, 256), 0), iota((256, 256), 1)
    back[0] = (c == ((r // 2) % 32) * 8 + (r // 64) * 2 + r % 2).astype(F32).astype(BF16)
    back[1] = (r == ((c // 2) % 32) * 8 + (c // 64) * 2 + c % 2).astype(F32).astype(BF16)

    def wait_all(ref, sem):
        pltpu.make_async_copy(ref, ref, sem).wait()

    def scatter(src, dst, m, ssem, rsem):
        def one(i, carry):
            t = peer(i)
            pltpu.make_async_remote_copy(
                src.at[t // 2], dst.at[m, chip], ssem, rsem, device_id=(s, t), device_id_type=MESH
            ).start()
            return carry

        pltpu.make_async_copy(src.at[chip], dst.at[m, chip], rsem).start()
        lax.fori_loop(1, CHIPS, one, 0)

    def sent(src, ssem):
        wait_all(src.at[pl.ds(0, CHIPS - 1)], ssem)

    def put(dst, value, w):
        dst[...] = value.reshape(CHIPS, 8, w).astype(BF16)

    def chunks(ref, m, w):
        return ref[m].astype(F32).reshape(256, w).astype(BF16)

    def dot(a, b):
        return jnp.dot(a, b, preferred_element_type=F32)

    def dispatch_forward(m):
        for p in range(PARTS):
            @pl.when((s != 0) | (m != 0))
            def _():
                wait_all(hbuf[p].at[m], h_recv[p].at[m])

            @pl.when(m > 0)
            def _():
                sent(send_df[p], df_s.at[p])

            put(send_df[p], dot(place[m], hbuf[p][m]), LANES[p])
            scatter(send_df[p], disp_f[p], m, df_s.at[p], df_r[p].at[m])

    def expert_forward(m):
        total = jnp.zeros((ROWS, 1), F32)
        for p in range(PARTS):
            w = LANES[p]
            wait_all(disp_f[p].at[m], df_r[p].at[m])
            rows = dot(back[0], chunks(disp_f[p], m, w))
            for q in range(4):
                block = rows[q * ROWS : (q + 1) * ROWS]
                total = total + jnp.sum(block * block, axis=1, keepdims=True)
                cols = slice(STARTS[p] + q * w, STARTS[p] + (q + 1) * w)
                hrows[m, :, cols] = block.astype(BF16)
                act[:, cols] = (block * gain_ref[0:1, cols]).astype(BF16)
            if p == 0:
                @pl.when(m == 0)
                def _():
                    for n in range(2):
                        local[n].wait()
                        shared[n].wait_recv()
            feats = slice(STARTS[p], STARTS[p] + 4 * w)

            def tile(i, carry):
                hf, at = i // 2, pl.ds(pl.multiple_of((i % 2) * TILE, TILE), TILE)
                to = pl.ds(pl.multiple_of(i * TILE, TILE), TILE)
                x = act[:, feats]
                a, b = dot(x, wg[hf, feats, at]), dot(x, wu[hf, feats, at])
                if p > 0:
                    a, b = a + acc_a[:, to], b + acc_b[:, to]
                acc_a[:, to] = a
                acc_b[:, to] = b
                return carry

            lax.fori_loop(0, 4, tile, 0)
        inv = lax.rsqrt(total * (1.0 / WIDTH) + EPS)
        rms_all[m] = jnp.broadcast_to(inv, (ROWS, 128))
        a, b = acc_a[...] * inv, acc_b[...] * inv
        gate_pre[m] = a
        up_pre[m] = b
        act[:, : 2 * HALF] = (a * jax.nn.sigmoid(a) * b).astype(BF16)

        @pl.when(m == 0)
        def _():
            local[2].wait()
            shared[2].wait_recv()

        for p in range(PARTS):
            w = LANES[p]
            blocks = []
            for q in range(4):
                cols = slice(STARTS[p] + q * w, STARTS[p] + (q + 1) * w)
                y = dot(act[:, :HALF], wd[0, :, cols]) + dot(act[:, HALF : 2 * HALF], wd[1, :, cols])
                blocks.append(y.astype(BF16))

            @pl.when(m > 0)
            def _():
                sent(send_cf[p], cf_s.at[p])

            put(send_cf[p], dot(back[1], jnp.concatenate(blocks, axis=0)), w)
            scatter(send_cf[p], coll_f[p], m, cf_s.at[p], cf_r[p].at[m])

    def combine_forward(m):
        for p in range(PARTS):
            w = LANES[p]
            wait_all(coll_f[p].at[m], cf_r[p].at[m])
            rows = dot(pick[m], chunks(coll_f[p], m, w))
            erows[p][m] = rows.astype(BF16)

            @pl.when(s < 3)
            def _():
                @pl.when((m > 0) | (s != 0))
                def _():
                    wait_all(hsend[p], h_ssem.at[p])

                hsend[p][...] = (hbuf[p][m].astype(F32) + gate_ref[m] * rows).astype(BF16)
                pltpu.make_async_remote_copy(
                    hsend[p], hbuf[p].at[m], h_ssem.at[p], h_recv[p].at[m],
                    device_id=(s + 1, me), device_id_type=MESH,
                ).start()

    def dispatch_backward(m):
        for p in range(PARTS):
            @pl.when((s != 3) | (m != 3))
            def _():
                wait_all(gbuf[p].at[m], g_recv[p].at[m])

            @pl.when(m > 0)
            def _():
                sent(send_db[p], db_s.at[p])

            grads = (gate_ref[m] * gbuf[p][m].astype(F32)).astype(BF16)
            put(send_db[p], dot(place[m], grads), LANES[p])
            scatter(send_db[p], disp_b[p], m, db_s.at[p], db_r[p].at[m])

    def expert_backward(m):
        for p in range(PARTS):
            w = LANES[p]
            wait_all(disp_b[p].at[m], db_r[p].at[m])
            rows = dot(back[0], chunks(disp_b[p], m, w)).astype(BF16)
            for q in range(4):
                act[:, STARTS[p] + q * w : STARTS[p] + (q + 1) * w] = rows[q * ROWS : (q + 1) * ROWS]
            feats = slice(STARTS[p], STARTS[p] + 4 * w)

            def tile(i, carry):
                hf, at = i // 2, pl.ds(pl.multiple_of((i % 2) * TILE, TILE), TILE)
                to = pl.ds(pl.multiple_of(i * TILE, TILE), TILE)
                a = lax.dot_general(act[:, feats], wd[hf, at, feats], NT, preferred_element_type=F32)
                if p > 0:
                    a = a + acc_a[:, to]
                acc_a[:, to] = a
                return carry

            lax.fori_loop(0, 4, tile, 0)
        a, b, d = gate_pre[m], up_pre[m], acc_a[...]
        sigma = jax.nn.sigmoid(a)
        grad_gate = (d * b * sigma * (1.0 + a * (1.0 - sigma))).astype(BF16)
        grad_up = (d * a * sigma).astype(BF16)
        act[:, : 2 * HALF] = grad_gate
        act[:, 2 * HALF : 4 * HALF] = grad_up
        inv = rms_all[m][:, :1]
        mixed = jnp.sum(grad_gate.astype(F32) * a + grad_up.astype(F32) * b, axis=1, keepdims=True)
        factor = inv * inv * mixed * (1.0 / WIDTH)
        for p in range(PARTS):
            w = LANES[p]
            blocks = []
            for q in range(4):
                cols = slice(STARTS[p] + q * w, STARTS[p] + (q + 1) * w)
                y = jnp.zeros((ROWS, w), F32)
                for n, weights in enumerate((wg, wu)):
                    for hf in range(2):
                        x = act[:, (2 * n + hf) * HALF : (2 * n + hf + 1) * HALF]
                        y = y + lax.dot_general(
                            x, weights[hf, cols, :], NT, preferred_element_type=F32
                        )
                y = y * inv * gain_ref[0:1, cols] - hrows[m, :, cols].astype(F32) * factor
                blocks.append(y.astype(BF16))

            @pl.when(m > 0)
            def _():
                sent(send_cb[p], cb_s.at[p])

            put(send_cb[p], dot(back[1], jnp.concatenate(blocks, axis=0)), w)
            scatter(send_cb[p], coll_b[p], m, cb_s.at[p], cb_r[p].at[m])

    def combine_backward(m):
        gates = jnp.zeros((128, 1), F32)
        for p in range(PARTS):
            w = LANES[p]
            wait_all(coll_b[p].at[m], cb_r[p].at[m])
            upper = gbuf[p][m].astype(F32)
            grads = (upper + dot(pick[m], chunks(coll_b[p], m, w))).astype(BF16)

            @pl.when(s > 0)
            def _():
                @pl.when((m > 0) | (s != 3))
                def _():
                    wait_all(gsend[p], g_ssem.at[p])

                gsend[p][...] = grads
                pltpu.make_async_remote_copy(
                    gsend[p], gbuf[p].at[m], g_ssem.at[p], g_recv[p].at[m],
                    device_id=(s - 1, me), device_id_type=MESH,
                ).start()

            for q in range(4):
                cols = slice(STARTS[p] + q * w, STARTS[p] + (q + 1) * w)
                gin_ref[0, m, :, cols] = grads[q * TOK : (q + 1) * TOK]
            gates = gates + jnp.sum(upper * erows[p][m].astype(F32), axis=1, keepdims=True)
        ggate_ref[0, m] = gates[:TOK] + gates[TOK : 2 * TOK] + gates[2 * TOK : 3 * TOK] + gates[3 * TOK :]

    lag = jnp.where(s == 3, 0, jnp.where(s == 2, 3, 5))

    def when_in(i, step):
        @pl.when((i >= 0) & (i < MICRO))
        def _():
            step(i)

    def tick(j, carry):
        when_in(j - lag, dispatch_backward)
        when_in(j, dispatch_forward)
        when_in(j - 1, combine_forward)
        when_in(j - lag - 1, combine_backward)
        when_in(j, expert_forward)
        when_in(j - lag, expert_backward)
        return carry

    lax.fori_loop(0, MICRO + 6, tick, 0)

    for p in range(PARTS):
        sent(send_df[p], df_s.at[p])
        sent(send_cf[p], cf_s.at[p])
        sent(send_db[p], db_s.at[p])
        sent(send_cb[p], cb_s.at[p])
        wait_all(hsend[p], h_ssem.at[p])
        wait_all(gsend[p], g_ssem.at[p])
    for n in range(3):
        shared[n].wait_send()


def body(tokens_in, cotangent, norm_gain, w_gate, w_up, w_down, expert_ids, gate_weights):
    tiled = jnp.tile(expert_ids[0, :, :, 0], (1, 4))
    gates = jnp.tile(gate_weights[0, :, :, 0], (1, 4))
    vmem = pl.BlockSpec(memory_space=pltpu.VMEM)
    hbm = pl.BlockSpec(memory_space=pl.ANY)
    dma = pltpu.SemaphoreType.DMA

    def parts(make):
        return tuple(make(w) for w in LANES)

    def home(count):
        return parts(lambda w: pltpu.VMEM((count, 128, w), BF16))

    def landing():
        return parts(lambda w: pltpu.VMEM((MICRO, CHIPS, 8, w), BF16))

    def sending():
        return parts(lambda w: pltpu.VMEM((CHIPS, 8, w), BF16))

    def per_micro():
        return tuple(dma((MICRO,)) for w in LANES)

    return pl.pallas_call(
        kernel,
        out_shape=(
            jax.ShapeDtypeStruct((1, MICRO, TOK, WIDTH), BF16),
            jax.ShapeDtypeStruct((1, MICRO, TOK, 1), F32),
        ),
        in_specs=[vmem, vmem, vmem, hbm, hbm, hbm, vmem, vmem, vmem],
        out_specs=(vmem, vmem),
        scratch_shapes=[
            pltpu.VMEM((2, WIDTH, HALF), BF16),
            pltpu.VMEM((2, WIDTH, HALF), BF16),
            pltpu.VMEM((2, HALF, WIDTH), BF16),
            pltpu.VMEM((MICRO, 256, 128), BF16),
            pltpu.VMEM((MICRO, 128, 256), BF16),
            pltpu.VMEM((2, 256, 256), BF16),
            home(MICRO), home(MICRO),
            landing(), landing(), landing(), landing(),
            sending(), sending(), sending(), sending(),
            parts(lambda w: pltpu.VMEM((128, w), BF16)),
            parts(lambda w: pltpu.VMEM((128, w), BF16)),
            home(MICRO),
            pltpu.VMEM((MICRO, ROWS, WIDTH), BF16),
            pltpu.VMEM((MICRO, ROWS, 2 * HALF), F32),
            pltpu.VMEM((MICRO, ROWS, 2 * HALF), F32),
            pltpu.VMEM((MICRO, ROWS, 128), F32),
            pltpu.VMEM((ROWS, 2 * HALF), F32),
            pltpu.VMEM((ROWS, 2 * HALF), F32),
            pltpu.VMEM((ROWS, WIDTH), BF16),
            dma((3,)), dma((3,)), dma((3,)),
            per_micro(), per_micro(), dma((PARTS,)), dma((PARTS,)),
            per_micro(), per_micro(), per_micro(), per_micro(),
            dma((PARTS,)), dma((PARTS,)), dma((PARTS,)), dma((PARTS,)),
        ],
        compiler_params=pltpu.CompilerParams(
            collective_id=0, has_side_effects=True, vmem_limit_bytes=60 * 1024 * 1024
        ),
        cost_estimate=pl.CostEstimate(
            flops=4 * 2 * 6 * 64 * 1024 * WIDTH, bytes_accessed=24 * 1024 * 1024, transcendentals=0
        ),
    )(
        tokens_in, cotangent, norm_gain, w_gate, w_up, w_down,
        tiled[:, None, :], tiled[:, :, None], gates[:, :, None],
    )


def solution(mesh):
    return jax.shard_map(
        body,
        mesh=mesh,
        in_specs=(
            P("section", "expert", None),
            P("section", "expert", None),
            P("section", None),
            P("section", "expert", None, None),
            P("section", "expert", None, None),
            P("section", "expert", None, None),
            P("section", None, "expert", None),
            P("section", None, "expert", None),
        ),
        out_specs=(P("section", None, "expert", None), P("section", None, "expert", None)),
        check_vma=False,
    )
```

```python
import functools

import jax
import jax.numpy as jnp
from jax import lax
from jax.experimental import pallas as pl
from jax.experimental.pallas import tpu as pltpu
from jax.sharding import PartitionSpec as P

MESH = pl.DeviceIdType.MESH
EPS = 1e-06
MICRO = 4
TOK = 32
CHIPS = 32
WIDTH = 3584
HALF = 512
HIDDEN = 2 * HALF
ROWS = 2 * CHIPS
LANE = 128
PART = 4 * LANE
PARTS = WIDTH // PART
F32 = jnp.float32
BF16 = jnp.bfloat16
NT = (((1,), (1,)), ((), ()))


def iota(shape, dim):
    return lax.broadcasted_iota(jnp.int32, shape, dim)


def dot(a, b):
    return jnp.dot(a, b, preferred_element_type=F32)


def dot_t(a, b):
    return lax.dot_general(a, b, NT, preferred_element_type=F32)


def kernel(
    tok_ref, cot_ref, gain_ref, wg_ref, wu_ref, wd_ref, id_ref, gw_ref,
    gin_ref, ggate_ref,
    wg, wu, wd, place, pick, back, gates,
    hbuf, gbuf, disp_f, disp_b, coll_f, coll_b, send_df, send_db, send_cf, send_cb,
    hsend, gsend, erows, hrows, gate_pre, up_pre, hidden, grad_act, rms_all, acc_a, acc_b, act,
    w_send, w_recv, w_local, h_recv, g_recv, h_ssem, g_ssem,
    df_r, db_r, cf_r, cb_r, df_s, db_s, cf_s, cb_s,
):
    s, me = lax.axis_index("section"), lax.axis_index("expert")
    chip, core = me // 2, me % 2
    cx, cz = chip // 8, chip % 8
    sibling = me + 1 - 2 * core

    columns = [((cx + i) % 4) * 16 + core for i in range(4)]
    layers = [((cz + i) % 8) * 2 for i in range(8)]

    def peer(i):
        return columns[i // 8] + layers[i % 8]

    local = []
    for n, (src, dst) in enumerate(((wg_ref, wg), (wu_ref, wu), (wd_ref, wd))):
        local.append(pltpu.make_async_copy(src.at[0, 0], dst.at[core], w_local.at[n]))
        local[-1].start()

    barrier = pltpu.get_barrier_semaphore()

    for i in range(1, CHIPS):
        pl.semaphore_signal(barrier, inc=1, device_id=(s, peer(i)), device_id_type=MESH)
    pl.semaphore_signal(barrier, inc=1, device_id=(s, sibling), device_id_type=MESH)
    for i in range(1, 4):
        pl.semaphore_signal(barrier, inc=1, device_id=((s + i) % 4, me), device_id_type=MESH)

    def stack(src, dst, p):
        for q in range(4):
            cols = slice(p * PART + q * LANE, p * PART + (q + 1) * LANE)
            dst[p, q * TOK : (q + 1) * TOK, :] = src[0, :, cols]

    for p in range(PARTS):
        @pl.when(s == 0)
        def _():
            stack(tok_ref, hbuf.at[0], p)

        @pl.when(s != 0)
        def _():
            stack(tok_ref, hsend, p)

        @pl.when(s == 3)
        def _():
            stack(cot_ref, gbuf.at[3], p)

        @pl.when(s != 3)
        def _():
            stack(cot_ref, gsend, p)

    def tables(m, carry):
        ti, tj = iota((128, TOK), 0), iota((128, TOK), 1)
        ids = jnp.sum(jnp.where(ti % TOK == tj, id_ref[0, m], 0), axis=1, keepdims=True)
        weights = jnp.sum(jnp.where(ti % TOK == tj, gw_ref[0, m], 0.0), axis=1, keepdims=True)
        gates[m] = jnp.broadcast_to(weights, (128, LANE))
        idcol = jnp.broadcast_to(ids, (128, 128))
        ti, tj = iota((128, 128), 0), iota((128, 128), 1)
        idrow = jnp.sum(jnp.where(ti == tj, idcol, 0), axis=0, keepdims=True)
        same = idcol == idrow
        before_row = same & (ti < TOK) & (ti < tj % TOK)
        before_col = same & (tj < TOK) & (tj < ti % TOK)
        slot_row = 2 * idrow + jnp.sum(before_row.astype(jnp.int32), axis=0, keepdims=True)
        slot_col = 2 * ids + jnp.sum(before_col.astype(jnp.int32), axis=1, keepdims=True)
        r, c = iota((256, 128), 0), iota((256, 128), 1)
        hit = ((r // 8) * 2 + r % 2 == slot_row) & ((r // 2) % 4 == c // TOK)
        place[m] = hit.astype(F32).astype(BF16)
        r, c = iota((128, 256), 1), iota((128, 256), 0)
        hit = ((r // 8) * 2 + r % 2 == slot_col) & ((r // 2) % 4 == c // TOK)
        pick[m] = hit.astype(F32).astype(BF16)
        return carry

    lax.fori_loop(0, MICRO, tables, 0)
    r, c = iota((256, 256), 0), iota((256, 256), 1)
    back[0] = (c == ((r // 2) % 32) * 8 + (r // 64) * 2 + r % 2).astype(F32).astype(BF16)
    back[1] = (r == ((c // 2) % 32) * 8 + (c // 64) * 2 + c % 2).astype(F32).astype(BF16)

    pl.semaphore_wait(barrier, CHIPS + 3)

    def hop(src, dst, ssem, rsem, to):
        pltpu.make_async_remote_copy(
            src, dst, ssem, rsem, device_id=(to, me), device_id_type=MESH
        ).start()

    def bring_tokens(p, carry):
        @pl.when(s != 0)
        def _():
            hop(hsend.at[p], hbuf.at[s, p], h_ssem.at[p], h_recv.at[s, p], 0)

        @pl.when(s != 3)
        def _():
            hop(gsend.at[p], gbuf.at[s, p], g_ssem.at[p], g_recv.at[s, p], 3)

        return carry

    lax.fori_loop(0, PARTS, bring_tokens, 0)

    shared = []
    for n, (src, dst) in enumerate(((wg_ref, wg), (wu_ref, wu), (wd_ref, wd))):
        shared.append(
            pltpu.make_async_remote_copy(
                src.at[0, 0], dst.at[core], w_send.at[n], w_recv.at[n],
                device_id=(s, sibling), device_id_type=MESH,
            )
        )
        shared[-1].start()

    def wait_all(ref, sem):
        pltpu.make_async_copy(ref, ref, sem).wait()

    def others(ref):
        return ref.at[pl.ds(0, CHIPS - 1)]

    def scatter(value, src, dst, ssem, rsem, m, p):
        @pl.when(m > 0)
        def _():
            wait_all(others(src.at[p]), ssem.at[p])

        src[p] = value.reshape(CHIPS, 8, LANE).astype(BF16)

        for i in range(1, CHIPS):
            t = peer(i)
            pltpu.make_async_remote_copy(
                src.at[p, t // 2], dst.at[m, p, chip], ssem.at[p], rsem.at[m, p],
                device_id=(s, t), device_id_type=MESH,
            ).start()
        dst[m, p, chip] = src[p, chip]

    def gathered(ref, sem, m, p):
        wait_all(others(ref.at[m, p]), sem.at[m, p])
        return chunks(ref, m, p)

    def chunks(ref, m, p):
        return ref[m, p].astype(F32).reshape(CHIPS * 8, LANE).astype(BF16)

    def features(p, q=0, size=PART):
        return pl.ds(pl.multiple_of(p * PART + q * LANE, LANE), size)

    def over_parts(step):
        def one(p, carry):
            step(p)
            return carry

        lax.fori_loop(0, PARTS, one, 0)

    def dispatch_forward(m, p):
        @pl.when((s != 0) | (m != 0))
        def _():
            wait_all(hbuf.at[m, p], h_recv.at[m, p])

        scatter(dot(place[m], hbuf[m, p]), send_df, disp_f, df_s, df_r, m, p)

    def expert_forward(m):
        @pl.when(m == 0)
        def _():
            for n in range(2):
                local[n].wait()
                shared[n].wait_recv()

        acc_a[...] = jnp.zeros_like(acc_a)
        acc_b[...] = jnp.zeros_like(acc_b)

        def one(p, total):
            rows = dot(back[0], gathered(disp_f, df_r, m, p))
            for q in range(4):
                block = rows[q * ROWS : (q + 1) * ROWS]
                total = total + block * block
                hrows[m, :, features(p, q, LANE)] = block.astype(BF16)
                act[:, q * LANE : (q + 1) * LANE] = (
                    block * gain_ref[0:1, features(p, q, LANE)]
                ).astype(BF16)
            for hf in range(2):
                to = slice(hf * HALF, (hf + 1) * HALF)
                acc_a[:, to] += dot(act[:, :PART], wg[hf, features(p), :])
                acc_b[:, to] += dot(act[:, :PART], wu[hf, features(p), :])
            return total

        total = lax.fori_loop(0, PARTS, one, jnp.zeros((ROWS, LANE), F32))
        inv = lax.rsqrt(jnp.sum(total, axis=1, keepdims=True) * (1.0 / WIDTH) + EPS)
        rms_all[m] = jnp.broadcast_to(inv, (ROWS, LANE))
        a, b = acc_a[...] * inv, acc_b[...] * inv
        gate_pre[m] = a
        up_pre[m] = b
        hidden[m] = (a * jax.nn.sigmoid(a) * b).astype(BF16)

        @pl.when(m == 0)
        def _():
            @pl.when(s != 3)
            def _():
                local[2].wait()
                shared[2].wait_recv()

    def expert_down(m):
        def one(p):
            y = dot(hidden[m, :, :HALF], wd[0, :, features(p)])
            y = (y + dot(hidden[m, :, HALF:], wd[1, :, features(p)])).astype(BF16)
            y = jnp.concatenate([y[:, q * LANE : (q + 1) * LANE] for q in range(4)], axis=0)
            scatter(dot(back[1], y), send_cf, coll_f, cf_s, cf_r, m, p)

        over_parts(one)

    def combine_forward(m, p):
        rows = dot(pick[m], gathered(coll_f, cf_r, m, p))
        erows[m, p] = rows.astype(BF16)

        @pl.when(s < 3)
        def _():
            @pl.when((m > 0) | (s != 0))
            def _():
                wait_all(hsend.at[p], h_ssem.at[p])

            hsend[p] = (hbuf[m, p].astype(F32) + gates[m] * rows).astype(BF16)
            hop(hsend.at[p], hbuf.at[m, p], h_ssem.at[p], h_recv.at[m, p], s + 1)

    def dispatch_backward(m, p):
        @pl.when((s != 3) | (m != 3))
        def _():
            wait_all(gbuf.at[m, p], g_recv.at[m, p])

        grads = (gates[m] * gbuf[m, p].astype(F32)).astype(BF16)
        scatter(dot(place[m], grads), send_db, disp_b, db_s, db_r, m, p)

    def expert_grad_act(m):
        @pl.when((m == 0) & (s == 3))
        def _():
            local[2].wait()
            shared[2].wait_recv()

        grad_act[m] = jnp.zeros((ROWS, HIDDEN), F32)

        def one(p):
            rows = dot(back[0], gathered(disp_b, db_r, m, p)).astype(BF16)
            for q in range(4):
                act[:, q * LANE : (q + 1) * LANE] = rows[q * ROWS : (q + 1) * ROWS]
            for hf in range(2):
                to = slice(hf * HALF, (hf + 1) * HALF)
                grad_act[m, :, to] += dot_t(act[:, :PART], wd[hf, :, features(p)])

        over_parts(one)

    def expert_backward(m):
        a, b, d = gate_pre[m], up_pre[m], grad_act[m]
        sigma = jax.nn.sigmoid(a)
        grad_gate = (d * b * sigma * (1.0 + a * (1.0 - sigma))).astype(BF16)
        grad_up = (d * a * sigma).astype(BF16)
        act[:, :HIDDEN] = grad_gate
        act[:, HIDDEN : 2 * HIDDEN] = grad_up
        inv = rms_all[m][:, :1]
        mixed = jnp.sum(grad_gate.astype(F32) * a + grad_up.astype(F32) * b, axis=1, keepdims=True)
        factor = inv * inv * mixed * (1.0 / WIDTH)

        def one(p):
            y = jnp.zeros((ROWS, PART), F32)
            for n, weights in enumerate((wg, wu)):
                for hf in range(2):
                    x = act[:, (2 * n + hf) * HALF : (2 * n + hf + 1) * HALF]
                    y = y + dot_t(x, weights[hf, features(p), :])
            y = y * inv * gain_ref[0:1, features(p)] - hrows[m, :, features(p)].astype(F32) * factor
            y = y.astype(BF16)
            y = jnp.concatenate([y[:, q * LANE : (q + 1) * LANE] for q in range(4)], axis=0)
            scatter(dot(back[1], y), send_cb, coll_b, cb_s, cb_r, m, p)

        over_parts(one)

    def combine_backward(m, p):
        delta = dot(pick[m], gathered(coll_b, cb_r, m, p))
        grads = (gbuf[m, p].astype(F32) + delta).astype(BF16)

        @pl.when(s > 0)
        def _():
            @pl.when((m > 0) | (s != 3))
            def _():
                wait_all(gsend.at[p], g_ssem.at[p])

            gsend[p] = grads
            hop(gsend.at[p], gbuf.at[m, p], g_ssem.at[p], g_recv.at[m, p], s - 1)

        for q in range(4):
            gin_ref[0, m, :, features(p, q, LANE)] = grads[q * TOK : (q + 1) * TOK]

    def gate_grads(m):
        def one(p, total):
            return total + gbuf[m, p].astype(F32) * erows[m, p].astype(F32)

        total = lax.fori_loop(0, PARTS, one, jnp.zeros((128, LANE), F32))
        total = total[:TOK] + total[TOK : 2 * TOK] + total[2 * TOK : 3 * TOK] + total[3 * TOK :]
        column = jnp.sum(total, axis=1, keepdims=True)
        diagonal = iota((TOK, TOK), 0) == iota((TOK, TOK), 1)
        ggate_ref[0, m] = jnp.sum(jnp.where(diagonal, column, 0.0), axis=0, keepdims=True)

    def begin(first, second, third, last):
        return jnp.where(s == 0, first, jnp.where(s == 1, second, jnp.where(s == 2, third, last)))

    forward = 4
    grads_in = begin(9, 9, 7, 0)
    grads_out = begin(9, 9, 7, 4)
    down = begin(4, 4, 4, 8)
    home = begin(5, 5, 5, 12)
    scores = begin(10, 10, 8, 12)

    def tick(j, carry):
        def when_in(start, step):
            @pl.when((j >= start) & (j < start + MICRO))
            def _():
                step(lax.rem(j + (16 - start), MICRO))

        def forward_moves(p):
            when_in(home, lambda m: combine_forward(m, p))
            when_in(forward, lambda m: dispatch_forward(m, p))

        def backward_moves(p):
            when_in(grads_out + 1, lambda m: combine_backward(m, p))
            when_in(grads_in, lambda m: dispatch_backward(m, p))

        @pl.when(((j >= forward) & (j <= forward + MICRO)) | (j >= home))
        def _():
            over_parts(forward_moves)

        @pl.when(j >= grads_in)
        def _():
            over_parts(backward_moves)

        when_in(forward, expert_forward)
        when_in(down, expert_down)
        when_in(grads_in, expert_grad_act)
        when_in(grads_out, expert_backward)
        when_in(scores, gate_grads)
        return carry

    lax.fori_loop(0, 16, tick, 0)

    def finish(p):
        for src, sem in ((send_df, df_s), (send_cf, cf_s), (send_db, db_s), (send_cb, cb_s)):
            wait_all(others(src.at[p]), sem.at[p])
        wait_all(hsend.at[p], h_ssem.at[p])
        wait_all(gsend.at[p], g_ssem.at[p])

    over_parts(finish)
    for n in range(3):
        shared[n].wait_send()


def body(tokens_in, cotangent, norm_gain, w_gate, w_up, w_down, expert_ids, gate_weights):
    vmem = pl.BlockSpec(memory_space=pltpu.VMEM)
    hbm = pl.BlockSpec(memory_space=pl.ANY)
    dma = pltpu.SemaphoreType.DMA
    home = pltpu.VMEM((MICRO, PARTS, 128, LANE), BF16)
    landing = pltpu.VMEM((MICRO, PARTS, CHIPS, 8, LANE), BF16)
    sending = pltpu.VMEM((PARTS, CHIPS, 8, LANE), BF16)
    wide = pltpu.VMEM((MICRO, ROWS, HIDDEN), F32)
    each, part = dma((MICRO, PARTS)), dma((PARTS,))
    grad_inputs, grad_gates = pl.pallas_call(
        kernel,
        out_shape=(
            jax.ShapeDtypeStruct((1, MICRO, TOK, WIDTH), BF16),
            jax.ShapeDtypeStruct((1, MICRO, 1, TOK), F32),
        ),
        in_specs=[vmem, vmem, vmem, hbm, hbm, hbm, vmem, vmem],
        out_specs=(vmem, vmem),
        scratch_shapes=[
            pltpu.VMEM((2, WIDTH, HALF), BF16),
            pltpu.VMEM((2, WIDTH, HALF), BF16),
            pltpu.VMEM((2, HALF, WIDTH), BF16),
            pltpu.VMEM((MICRO, 256, 128), BF16),
            pltpu.VMEM((MICRO, 128, 256), BF16),
            pltpu.VMEM((2, 256, 256), BF16),
            pltpu.VMEM((MICRO, 128, LANE), F32),
            home, home,
            landing, landing, landing, landing,
            sending, sending, sending, sending,
            pltpu.VMEM((PARTS, 128, LANE), BF16),
            pltpu.VMEM((PARTS, 128, LANE), BF16),
            home,
            pltpu.VMEM((MICRO, ROWS, WIDTH), BF16),
            wide, wide,
            pltpu.VMEM((MICRO, ROWS, HIDDEN), BF16),
            wide,
            pltpu.VMEM((MICRO, ROWS, LANE), F32),
            pltpu.VMEM((ROWS, HIDDEN), F32),
            pltpu.VMEM((ROWS, HIDDEN), F32),
            pltpu.VMEM((ROWS, 2 * HIDDEN), BF16),
            dma((3,)), dma((3,)), dma((3,)),
            each, each, part, part,
            each, each, each, each,
            part, part, part, part,
        ],
        compiler_params=pltpu.CompilerParams(
            collective_id=0, has_side_effects=True, vmem_limit_bytes=60 * 1024 * 1024
        ),
        cost_estimate=pl.CostEstimate(
            flops=4 * 2 * 6 * 64 * 1024 * WIDTH, bytes_accessed=24 * 1024 * 1024, transcendentals=0
        ),
    )(
        tokens_in, cotangent, norm_gain, w_gate, w_up, w_down,
        jnp.swapaxes(expert_ids, 2, 3), jnp.swapaxes(gate_weights, 2, 3),
    )
    return grad_inputs, jnp.swapaxes(grad_gates, 2, 3)


def solution(mesh):
    return jax.shard_map(
        body,
        mesh=mesh,
        in_specs=(
            P("section", "expert", None),
            P("section", "expert", None),
            P("section", None),
            P("section", "expert", None, None),
            P("section", "expert", None, None),
            P("section", "expert", None, None),
            P("section", None, "expert", None),
            P("section", None, "expert", None),
        ),
        out_specs=(P("section", None, "expert", None), P("section", None, "expert", None)),
        check_vma=False,
    )
```

```python
import functools

import jax
import jax.numpy as jnp
from jax import lax
from jax.experimental import pallas as pl
from jax.experimental.pallas import tpu as pltpu
from jax.sharding import PartitionSpec as P

MESH = pl.DeviceIdType.MESH
EPS = 1e-06
MICRO = 4
TOK = 32
CHIPS = 32
WIDTH = 3584
HALF = 512
HIDDEN = 2 * HALF
ROWS = 2 * CHIPS
LANE = 128
PART = 4 * LANE
PARTS = WIDTH // PART
F32 = jnp.float32
BF16 = jnp.bfloat16
NT = (((1,), (1,)), ((), ()))


def iota(shape, dim):
    return lax.broadcasted_iota(jnp.int32, shape, dim)


def dot(a, b):
    return jnp.dot(a, b, preferred_element_type=F32)


def dot_t(a, b):
    return lax.dot_general(a, b, NT, preferred_element_type=F32)


def kernel(
    tok_ref, cot_ref, gain_ref, wg_ref, wu_ref, wd_ref, id_ref, gw_ref,
    gin_ref, ggate_ref,
    wg, wu, wd, place, pick, back, gates,
    hbuf, gbuf, disp_f, disp_b, coll_f, coll_b, send_df, send_db, send_cf, send_cb,
    hsend, gsend, erows, hrows, gate_pre, up_pre, hidden, grad_act, rms_all, acc_a, acc_b, act,
    w_send, w_recv, w_local, h_recv, g_recv, h_ssem, g_ssem,
    df_r, db_r, cf_r, cb_r, df_s, db_s, cf_s, cb_s,
):
    s, me = lax.axis_index("section"), lax.axis_index("expert")
    chip, core = me // 2, me % 2
    cx, cz = chip // 8, chip % 8
    sibling = me + 1 - 2 * core

    columns = [((cx + i) % 4) * 16 + core for i in range(4)]
    layers = [((cz + i) % 8) * 2 for i in range(8)]

    def peer(i):
        return columns[i // 8] + layers[i % 8]

    local = []
    for n, (src, dst) in enumerate(((wg_ref, wg), (wu_ref, wu), (wd_ref, wd))):
        local.append(pltpu.make_async_copy(src.at[0, 0], dst.at[core], w_local.at[n]))
        local[-1].start()

    barrier = pltpu.get_barrier_semaphore()

    for i in range(1, CHIPS):
        pl.semaphore_signal(barrier, inc=1, device_id=(s, peer(i)), device_id_type=MESH)
    pl.semaphore_signal(barrier, inc=1, device_id=(s, sibling), device_id_type=MESH)
    for i in range(1, 4):
        pl.semaphore_signal(barrier, inc=1, device_id=((s + i) % 4, me), device_id_type=MESH)

    def stack(src, dst, p):
        for q in range(4):
            cols = slice(p * PART + q * LANE, p * PART + (q + 1) * LANE)
            dst[p, q * TOK : (q + 1) * TOK, :] = src[0, :, cols]

    for p in range(PARTS):
        @pl.when(s == 0)
        def _():
            stack(tok_ref, hbuf.at[0], p)

        @pl.when(s != 0)
        def _():
            stack(tok_ref, hsend, p)

        @pl.when(s == 3)
        def _():
            stack(cot_ref, gbuf.at[3], p)

        @pl.when(s != 3)
        def _():
            stack(cot_ref, gsend, p)

    def tables(m, carry):
        ti, tj = iota((128, TOK), 0), iota((128, TOK), 1)
        ids = jnp.sum(jnp.where(ti % TOK == tj, id_ref[0, m], 0), axis=1, keepdims=True)
        weights = jnp.sum(jnp.where(ti % TOK == tj, gw_ref[0, m], 0.0), axis=1, keepdims=True)
        gates[m] = jnp.broadcast_to(weights, (128, LANE))
        idcol = jnp.broadcast_to(ids, (128, 128))
        ti, tj = iota((128, 128), 0), iota((128, 128), 1)
        idrow = jnp.sum(jnp.where(ti == tj, idcol, 0), axis=0, keepdims=True)
        same = idcol == idrow
        before_row = same & (ti < TOK) & (ti < tj % TOK)
        before_col = same & (tj < TOK) & (tj < ti % TOK)
        slot_row = 2 * idrow + jnp.sum(before_row.astype(jnp.int32), axis=0, keepdims=True)
        slot_col = 2 * ids + jnp.sum(before_col.astype(jnp.int32), axis=1, keepdims=True)
        r, c = iota((256, 128), 0), iota((256, 128), 1)
        hit = ((r // 8) * 2 + r % 2 == slot_row) & ((r // 2) % 4 == c // TOK)
        place[m] = hit.astype(F32).astype(BF16)
        r, c = iota((128, 256), 1), iota((128, 256), 0)
        hit = ((r // 8) * 2 + r % 2 == slot_col) & ((r // 2) % 4 == c // TOK)
        pick[m] = hit.astype(F32).astype(BF16)
        return carry

    lax.fori_loop(0, MICRO, tables, 0)
    r, c = iota((256, 256), 0), iota((256, 256), 1)
    back[0] = (c == ((r // 2) % 32) * 8 + (r // 64) * 2 + r % 2).astype(F32).astype(BF16)
    back[1] = (r == ((c // 2) % 32) * 8 + (c // 64) * 2 + c % 2).astype(F32).astype(BF16)

    pl.semaphore_wait(barrier, CHIPS + 3)

    def hop(src, dst, ssem, rsem, to):
        pltpu.make_async_remote_copy(
            src, dst, ssem, rsem, device_id=(to, me), device_id_type=MESH
        ).start()

    def bring_tokens(p, carry):
        @pl.when(s != 0)
        def _():
            hop(hsend.at[p], hbuf.at[s, p], h_ssem.at[p], h_recv.at[s, p], 0)

        @pl.when(s != 3)
        def _():
            hop(gsend.at[p], gbuf.at[s, p], g_ssem.at[p], g_recv.at[s, p], 3)

        return carry

    lax.fori_loop(0, PARTS, bring_tokens, 0)

    shared = []
    for n, (src, dst) in enumerate(((wg_ref, wg), (wu_ref, wu), (wd_ref, wd))):
        shared.append(
            pltpu.make_async_remote_copy(
                src.at[0, 0], dst.at[core], w_send.at[n], w_recv.at[n],
                device_id=(s, sibling), device_id_type=MESH,
            )
        )
        shared[-1].start()

    def wait_all(ref, sem):
        pltpu.make_async_copy(ref, ref, sem).wait()

    def others(ref):
        return ref.at[pl.ds(0, CHIPS - 1)]

    def scatter(value, src, dst, ssem, rsem, m, p):
        @pl.when(m > 0)
        def _():
            wait_all(others(src.at[p]), ssem.at[p])

        src[p] = value.reshape(CHIPS, 8, LANE).astype(BF16)

        for i in range(1, CHIPS):
            t = peer(i)
            pltpu.make_async_remote_copy(
                src.at[p, t // 2], dst.at[m, p, chip], ssem.at[p], rsem.at[m, p],
                device_id=(s, t), device_id_type=MESH,
            ).start()
        dst[m, p, chip] = src[p, chip]

    def gathered(ref, sem, m, p):
        wait_all(others(ref.at[m, p]), sem.at[m, p])
        return chunks(ref, m, p)

    def chunks(ref, m, p):
        return ref[m, p].astype(F32).reshape(CHIPS * 8, LANE).astype(BF16)

    def features(p, q=0, size=PART):
        return pl.ds(pl.multiple_of(p * PART + q * LANE, LANE), size)

    def over_parts(step, unroll=False):
        def one(p, carry):
            step(p)
            return carry

        lax.fori_loop(0, PARTS, one, 0, unroll=unroll)

    def dispatch_forward(m, p):
        @pl.when((s != 0) | (m != 0))
        def _():
            wait_all(hbuf.at[m, p], h_recv.at[m, p])

        scatter(dot(place[m], hbuf[m, p]), send_df, disp_f, df_s, df_r, m, p)

    def expert_forward(m):
        @pl.when(m == 0)
        def _():
            for n in range(2):
                local[n].wait()
                shared[n].wait_recv()

        acc_a[...] = jnp.zeros_like(acc_a)
        acc_b[...] = jnp.zeros_like(acc_b)

        def one(p, total):
            rows = dot(back[0], gathered(disp_f, df_r, m, p))
            for q in range(4):
                block = rows[q * ROWS : (q + 1) * ROWS]
                total = total + block * block
                hrows[m, :, features(p, q, LANE)] = block.astype(BF16)
                act[:, q * LANE : (q + 1) * LANE] = (
                    block * gain_ref[0:1, features(p, q, LANE)]
                ).astype(BF16)
            for hf in range(2):
                to = slice(hf * HALF, (hf + 1) * HALF)
                acc_a[:, to] += dot(act[:, :PART], wg[hf, features(p), :])
                acc_b[:, to] += dot(act[:, :PART], wu[hf, features(p), :])
            return total

        total = lax.fori_loop(0, PARTS, one, jnp.zeros((ROWS, LANE), F32), unroll=True)
        inv = lax.rsqrt(jnp.sum(total, axis=1, keepdims=True) * (1.0 / WIDTH) + EPS)
        rms_all[m] = jnp.broadcast_to(inv, (ROWS, LANE))
        a, b = acc_a[...] * inv, acc_b[...] * inv
        gate_pre[m] = a
        up_pre[m] = b
        hidden[m] = (a * jax.nn.sigmoid(a) * b).astype(BF16)

        @pl.when(m == 0)
        def _():
            @pl.when(s != 3)
            def _():
                local[2].wait()
                shared[2].wait_recv()

    def expert_down(m):
        def one(p):
            y = dot(hidden[m, :, :HALF], wd[0, :, features(p)])
            y = (y + dot(hidden[m, :, HALF:], wd[1, :, features(p)])).astype(BF16)
            y = jnp.concatenate([y[:, q * LANE : (q + 1) * LANE] for q in range(4)], axis=0)
            scatter(dot(back[1], y), send_cf, coll_f, cf_s, cf_r, m, p)

        over_parts(one, True)

    def combine_forward(m, p):
        rows = dot(pick[m], gathered(coll_f, cf_r, m, p))
        erows[m, p] = rows.astype(BF16)

        @pl.when(s < 3)
        def _():
            @pl.when((m > 0) | (s != 0))
            def _():
                wait_all(hsend.at[p], h_ssem.at[p])

            hsend[p] = (hbuf[m, p].astype(F32) + gates[m] * rows).astype(BF16)
            hop(hsend.at[p], hbuf.at[m, p], h_ssem.at[p], h_recv.at[m, p], s + 1)

    def dispatch_backward(m, p):
        @pl.when((s != 3) | (m != 3))
        def _():
            wait_all(gbuf.at[m, p], g_recv.at[m, p])

        grads = (gates[m] * gbuf[m, p].astype(F32)).astype(BF16)
        scatter(dot(place[m], grads), send_db, disp_b, db_s, db_r, m, p)

    def expert_grad_act(m):
        @pl.when((m == 0) & (s == 3))
        def _():
            local[2].wait()
            shared[2].wait_recv()

        grad_act[m] = jnp.zeros((ROWS, HIDDEN), F32)

        def one(p):
            rows = dot(back[0], gathered(disp_b, db_r, m, p)).astype(BF16)
            for q in range(4):
                act[:, q * LANE : (q + 1) * LANE] = rows[q * ROWS : (q + 1) * ROWS]
            for hf in range(2):
                to = slice(hf * HALF, (hf + 1) * HALF)
                grad_act[m, :, to] += dot_t(act[:, :PART], wd[hf, :, features(p)])

        over_parts(one, True)

    def expert_backward(m):
        a, b, d = gate_pre[m], up_pre[m], grad_act[m]
        sigma = jax.nn.sigmoid(a)
        grad_gate = (d * b * sigma * (1.0 + a * (1.0 - sigma))).astype(BF16)
        grad_up = (d * a * sigma).astype(BF16)
        act[:, :HIDDEN] = grad_gate
        act[:, HIDDEN : 2 * HIDDEN] = grad_up
        inv = rms_all[m][:, :1]
        mixed = jnp.sum(grad_gate.astype(F32) * a + grad_up.astype(F32) * b, axis=1, keepdims=True)
        factor = inv * inv * mixed * (1.0 / WIDTH)

        def one(p):
            y = jnp.zeros((ROWS, PART), F32)
            for n, weights in enumerate((wg, wu)):
                for hf in range(2):
                    x = act[:, (2 * n + hf) * HALF : (2 * n + hf + 1) * HALF]
                    y = y + dot_t(x, weights[hf, features(p), :])
            y = y * inv * gain_ref[0:1, features(p)] - hrows[m, :, features(p)].astype(F32) * factor
            y = y.astype(BF16)
            y = jnp.concatenate([y[:, q * LANE : (q + 1) * LANE] for q in range(4)], axis=0)
            scatter(dot(back[1], y), send_cb, coll_b, cb_s, cb_r, m, p)

        over_parts(one, True)

    def combine_backward(m, p):
        delta = dot(pick[m], gathered(coll_b, cb_r, m, p))
        grads = (gbuf[m, p].astype(F32) + delta).astype(BF16)

        @pl.when(s > 0)
        def _():
            @pl.when((m > 0) | (s != 3))
            def _():
                wait_all(gsend.at[p], g_ssem.at[p])

            gsend[p] = grads
            hop(gsend.at[p], gbuf.at[m, p], g_ssem.at[p], g_recv.at[m, p], s - 1)

        for q in range(4):
            gin_ref[0, m, :, features(p, q, LANE)] = grads[q * TOK : (q + 1) * TOK]

    def gate_grads(m):
        def one(p, total):
            return total + gbuf[m, p].astype(F32) * erows[m, p].astype(F32)

        total = lax.fori_loop(0, PARTS, one, jnp.zeros((128, LANE), F32))
        total = total[:TOK] + total[TOK : 2 * TOK] + total[2 * TOK : 3 * TOK] + total[3 * TOK :]
        column = jnp.sum(total, axis=1, keepdims=True)
        diagonal = iota((TOK, TOK), 0) == iota((TOK, TOK), 1)
        ggate_ref[0, m] = jnp.sum(jnp.where(diagonal, column, 0.0), axis=0, keepdims=True)

    def begin(first, second, third, last):
        return jnp.where(s == 0, first, jnp.where(s == 1, second, jnp.where(s == 2, third, last)))

    forward = 4
    tokens_out = begin(3, 4, 4, 4)
    grads_in = begin(9, 9, 6, 0)
    grads_out = begin(9, 9, 6, 4)
    down = begin(4, 4, 4, 8)
    home = begin(5, 5, 5, 12)
    scores = begin(10, 10, 7, 12)

    def tick(j, carry):
        def when_in(start, step):
            @pl.when((j >= start) & (j < start + MICRO))
            def _():
                step(lax.rem(j + (16 - start), MICRO))

        def forward_moves(p):
            when_in(tokens_out, lambda m: dispatch_forward(m, p))

        def forward_home(m):
            over_parts(lambda p: combine_forward(m, p))

        def backward_moves(p):
            when_in(grads_out + 1, lambda m: combine_backward(m, p))
            when_in(grads_in, lambda m: dispatch_backward(m, p))

        when_in(home, forward_home)

        @pl.when((j >= tokens_out) & (j <= forward + MICRO))
        def _():
            over_parts(forward_moves)

        @pl.when(j >= grads_in)
        def _():
            over_parts(backward_moves)

        when_in(forward, expert_forward)
        when_in(down, expert_down)
        when_in(grads_in, expert_grad_act)
        when_in(grads_out, expert_backward)
        when_in(scores, gate_grads)
        return carry

    lax.fori_loop(0, 16, tick, 0)

    def finish(p):
        for src, sem in ((send_df, df_s), (send_cf, cf_s), (send_db, db_s), (send_cb, cb_s)):
            wait_all(others(src.at[p]), sem.at[p])
        wait_all(hsend.at[p], h_ssem.at[p])
        wait_all(gsend.at[p], g_ssem.at[p])

    over_parts(finish)
    for n in range(3):
        shared[n].wait_send()


def body(tokens_in, cotangent, norm_gain, w_gate, w_up, w_down, expert_ids, gate_weights):
    vmem = pl.BlockSpec(memory_space=pltpu.VMEM)
    hbm = pl.BlockSpec(memory_space=pl.ANY)
    dma = pltpu.SemaphoreType.DMA
    home = pltpu.VMEM((MICRO, PARTS, 128, LANE), BF16)
    landing = pltpu.VMEM((MICRO, PARTS, CHIPS, 8, LANE), BF16)
    sending = pltpu.VMEM((PARTS, CHIPS, 8, LANE), BF16)
    wide = pltpu.VMEM((MICRO, ROWS, HIDDEN), F32)
    each, part = dma((MICRO, PARTS)), dma((PARTS,))
    grad_inputs, grad_gates = pl.pallas_call(
        kernel,
        out_shape=(
            jax.ShapeDtypeStruct((1, MICRO, TOK, WIDTH), BF16),
            jax.ShapeDtypeStruct((1, MICRO, 1, TOK), F32),
        ),
        in_specs=[vmem, vmem, vmem, hbm, hbm, hbm, vmem, vmem],
        out_specs=(vmem, vmem),
        scratch_shapes=[
            pltpu.VMEM((2, WIDTH, HALF), BF16),
            pltpu.VMEM((2, WIDTH, HALF), BF16),
            pltpu.VMEM((2, HALF, WIDTH), BF16),
            pltpu.VMEM((MICRO, 256, 128), BF16),
            pltpu.VMEM((MICRO, 128, 256), BF16),
            pltpu.VMEM((2, 256, 256), BF16),
            pltpu.VMEM((MICRO, 128, LANE), F32),
            home, home,
            landing, landing, landing, landing,
            sending, sending, sending, sending,
            pltpu.VMEM((PARTS, 128, LANE), BF16),
            pltpu.VMEM((PARTS, 128, LANE), BF16),
            home,
            pltpu.VMEM((MICRO, ROWS, WIDTH), BF16),
            wide, wide,
            pltpu.VMEM((MICRO, ROWS, HIDDEN), BF16),
            wide,
            pltpu.VMEM((MICRO, ROWS, LANE), F32),
            pltpu.VMEM((ROWS, HIDDEN), F32),
            pltpu.VMEM((ROWS, HIDDEN), F32),
            pltpu.VMEM((ROWS, 2 * HIDDEN), BF16),
            dma((3,)), dma((3,)), dma((3,)),
            each, each, part, part,
            each, each, each, each,
            part, part, part, part,
        ],
        compiler_params=pltpu.CompilerParams(
            collective_id=0, has_side_effects=True, vmem_limit_bytes=60 * 1024 * 1024
        ),
        cost_estimate=pl.CostEstimate(
            flops=4 * 2 * 6 * 64 * 1024 * WIDTH, bytes_accessed=24 * 1024 * 1024, transcendentals=0
        ),
    )(
        tokens_in, cotangent, norm_gain, w_gate, w_up, w_down,
        jnp.swapaxes(expert_ids, 2, 3), jnp.swapaxes(gate_weights, 2, 3),
    )
    return grad_inputs, jnp.swapaxes(grad_gates, 2, 3)


def solution(mesh):
    return jax.shard_map(
        body,
        mesh=mesh,
        in_specs=(
            P("section", "expert", None),
            P("section", "expert", None),
            P("section", None),
            P("section", "expert", None, None),
            P("section", "expert", None, None),
            P("section", "expert", None, None),
            P("section", None, "expert", None),
            P("section", None, "expert", None),
        ),
        out_specs=(P("section", None, "expert", None), P("section", None, "expert", None)),
        check_vma=False,
    )
```
